32 devices in a mesh: tm: 4 (over z), expert: 8 (over y, x, core).
Axes of the slice: x: 2, y: 2, z: 4, core: 2. Of those that a mesh axis runs over, the one named last changes fastest.
Arguments:
- x_in: float32 [8, 1024, 1024], P('expert', 'tm'), may hold values from -6 to 6
- z_gate: bfloat16 [8, 1024, 1024], P('expert', 'tm'), may hold values from -6 to 6
- b_proj: float32 [8, 1024, 128], P('expert', 'tm'), may hold values from -1.5 to 1.5
- c_proj: float32 [8, 1024, 128], P('expert', 'tm'), may hold values from -1.5 to 1.5
- decay_log: float32 [8, 1024, 16], P('expert', 'tm'), as said below
- skip_gain: float32 [16], replicated, may hold values from 0.5 to 2
- residual: float32 [8, 1024, 1024], P('expert', 'tm'), may hold values from -6 to 6
- ssd_gain: float32 [1024], replicated, may hold values from 0.5 to 1.5
- moe_gain: float32 [1024], replicated, may hold values from 0.5 to 1.5
- w_gate: bfloat16 [8, 1024, 1536], P('expert', 'tm'), may hold values from -0.1875 to 0.1875
- w_up: bfloat16 [8, 1024, 1536], P('expert', 'tm'), may hold values from -0.1875 to 0.1875
- w_down: bfloat16 [8, 1536, 1024], P('expert', 'tm'), may hold values from -0.15625 to 0.15625
- routes: int32 [8, 1024, 2], P('expert', 'tm'), may hold values from 0 to 7, all different within a row; in each aligned block of 256 rows (0 to 255, 256 to 511, ..., all dimensions but the last counted through in order) at most 96 rows name the same one
- route_weights: float32 [8, 1024, 2], P('expert', 'tm'), may hold values from 0.2 to 1
Outputs:
- mixed: float32 [8, 1024, 1024], P('expert', 'tm')
The draws below stay inside these ranges and needn't reach their ends.
Inputs may be any that keep to these rules, and one draw needn't show every extreme that they name: `routes`: the two experts of a time step differ. Among the time steps of one device no expert is named more than 96 times, and in every draw some device names some expert exactly 96 times. `decay_log`: every entry is at most zero.
All inputs are finite; a program needn't handle non-finite values.
Results may differ from the reference program's by a relative error of at most 0.0021.
Values may be sent and summed in bfloat16 or wider, within the bound.
A program may use at most 64 MiB of HBM per device.

```python
import math
import jax
import jax.numpy as jnp
import numpy as np
from jax import lax

D = 1024
HEADS = 16
STATE = 128
FF = 1536
L_DEV = 256
SEQ = 1024
SEQS = 8
EXPERTS = 8
CAP = 96


def draw_decay_log(key, part):
    keys = jax.random.split(key, 7)
    cutoff = 5
    quick = jax.random.randint(keys[0], (HEADS,), 0, 10) < cutoff
    quick_rate = jnp.exp(jax.random.uniform(keys[1], (HEADS,), jnp.float32, math.log(1.0 / 50.0), math.log(1.0 / 30.0)))
    slow_rate = jnp.exp(jax.random.uniform(keys[2], (HEADS,), jnp.float32, math.log(0.1), math.log(0.5))) / SEQ
    rates = jnp.where(quick, quick_rate, slow_rate)
    blocks = SEQ // L_DEV
    block_factor = jnp.exp(jax.random.uniform(keys[3], (SEQS, blocks, 1, HEADS), jnp.float32, math.log(0.5), math.log(2.0)))
    block_factor = jnp.broadcast_to(block_factor, (SEQS, blocks, L_DEV, HEADS)).reshape(SEQS, SEQ, HEADS)
    step_factor = jnp.exp(jax.random.uniform(keys[4], (SEQS, SEQ, HEADS), jnp.float32, math.log(0.5), math.log(2.0)))
    spots = jax.random.randint(keys[5], (SEQS, 3), 0, SEQ)
    places = jnp.any(jnp.arange(SEQ)[None, None, :] == spots[:, :, None], axis=1)
    losses = jnp.log(jax.random.uniform(keys[6], (SEQS, SEQ, HEADS), jnp.float32, 0.5, 0.8))
    return -rates[None, None, :] * block_factor * step_factor + jnp.where(places[:, :, None], losses, 0.0)


def block_levels(rng, shape, shards, least, largest):
    factor_of, own = 1.0, jax.random.fold_in(rng, 6)
    for dim, shards_of in shards:
        heights = jnp.exp(jax.random.uniform(jax.random.fold_in(own, dim), (shards_of,), jnp.float32, least / len(shards), largest / len(shards)))
        factor_of = factor_of * jnp.repeat(heights, shape[dim] // shards_of).reshape([-1 if axis == dim else 1 for axis in range(len(shape))])
    return factor_of


def routed_block(rng, own, number, rows, amount, top, most, lean):
    ranking = jax.random.permutation(rng, amount)
    heavy_load, usual = shares(amount, rows * top, most, lean, True), shares(amount, rows * top, most, lean, False)
    places = jnp.arange(amount)

    def named(sizes, offset_by):
        used = int((sizes > 0).sum())
        fixed = max(1, used // 4)
        moved = fixed + (places - fixed + offset_by * (used - fixed)) % max(1, amount - fixed)
        return jnp.zeros((amount,), jnp.int32).at[ranking[jnp.where(places < fixed, places, moved)]].set(jnp.asarray(sizes, jnp.int32))

    sizes = jnp.where(number % 4 == 0, named(heavy_load, number // 4), named(usual, number - number // 4 - 1))
    mixed = jax.random.permutation(jax.random.fold_in(own, 3), amount)
    donor, receiver = mixed[0:amount // 2 * 2:2], mixed[1:amount // 2 * 2:2]
    slack = jnp.minimum(sizes[donor] - 1, most - sizes[receiver]) // 2
    slack = jnp.where((donor == ranking[0]) | (receiver == ranking[0]) | (sizes[receiver] == 0), 0, jnp.maximum(slack, 0))
    moved = jax.random.randint(jax.random.fold_in(own, 4), (amount // 2,), 0, 1 << 20) % (slack + 1)
    sizes = sizes.at[donor].add(-moved).at[receiver].add(moved)
    members = jnp.searchsorted(jnp.cumsum(sizes), jnp.arange(rows * top), side="right").astype(jnp.int32)
    grid = members.reshape(top, rows).T
    grid = grid[jax.random.permutation(jax.random.fold_in(own, 1), rows)]
    offset_by = jax.random.randint(jax.random.fold_in(own, 2), (rows, 1), 0, top)
    return jnp.take_along_axis(grid, (jnp.arange(top)[None, :] + offset_by) % top, axis=1)


def shares(count, total, limit, skew, full):
    weights = [(1 << 20) // math.isqrt(standing ** skew) + 1 for standing in range(1, count + 1)]
    largest = limit if full else min(limit, max(-(-total // count), total * weights[0] // sum(weights)))
    least = 1 if total - largest >= count - 1 else 0
    counts, rest = [largest] + [least] * (count - 1), total - largest - least * (count - 1)
    while rest > 0:
        movable = [i for i in range(1, count) if counts[i] < largest] or [i for i in range(1, count) if counts[i] < limit]
        mass, remaining = sum([weights[i] for i in movable]), rest
        for i in movable:
            more = min(limit - counts[i], max(1, remaining * weights[i] // mass), rest)
            counts[i] = counts[i] + more
            rest = rest - more
    return np.array(counts)


def gaussian(stream_key, dims, deviation, most, cuts=(), held_as=jnp.bfloat16):
    entries = deviation * jax.random.normal(stream_key, dims, jnp.float32)
    if cuts:
        entries = entries * block_levels(stream_key, dims, cuts, -0.22, 0.18)
    return jnp.clip(entries, -most, most).astype(held_as)


def setup_inputs(seed: int = 0) -> dict:
    arg_keys = jax.random.split(jax.random.key(seed), 15)
    x_in = gaussian(arg_keys[0], (SEQS, SEQ, D), 1.0, 6.0, ((0, 8), (1, 4)), jnp.float32)
    z_gate = gaussian(arg_keys[1], (SEQS, SEQ, D), 1.0, 6.0, ((0, 8), (1, 4)))
    b_proj = gaussian(arg_keys[2], (SEQS, SEQ, STATE), 0.25, 1.5, ((0, 8), (1, 4)), jnp.float32)
    c_proj = gaussian(arg_keys[3], (SEQS, SEQ, STATE), 0.25, 1.5, ((0, 8), (1, 4)), jnp.float32)
    decay_log = draw_decay_log(jax.random.fold_in(arg_keys[14], 71), 0)
    skip_gain = jnp.clip(jnp.exp(jax.random.uniform(arg_keys[5], (HEADS,), jnp.float32, math.log(0.5), math.log(2.0))), 0.5, 2.0)
    residual = gaussian(arg_keys[6], (SEQS, SEQ, D), 1.0, 6.0, ((0, 8), (1, 4)), jnp.float32)
    ssd_gain = jnp.clip(1.0 + 0.1 * jax.random.normal(arg_keys[7], (D,), jnp.float32), 0.5, 1.5)
    moe_gain = jnp.clip(1.0 + 0.1 * jax.random.normal(arg_keys[8], (D,), jnp.float32), 0.5, 1.5)
    w_gate = gaussian(arg_keys[9], (EXPERTS, D, FF), D ** -0.5, 0.1875, ((0, 8), (1, 4)))
    w_up = gaussian(arg_keys[10], (EXPERTS, D, FF), D ** -0.5, 0.1875, ((0, 8), (1, 4)))
    w_down = gaussian(arg_keys[11], (EXPERTS, FF, D), FF ** -0.5, 0.15625, ((0, 8), (1, 4)))
    routes_keys = jax.random.split(jax.random.fold_in(arg_keys[12], 1), SEQS * SEQ // L_DEV)
    routes_turns = jax.random.permutation(jax.random.fold_in(arg_keys[12], 3), SEQS * SEQ // L_DEV)
    routes = jax.vmap(lambda own, number: routed_block(jax.random.fold_in(arg_keys[12], 2), own, number, L_DEV, EXPERTS, 2, CAP, 2))(routes_keys, routes_turns).reshape((SEQS, SEQ, 2))
    route_weights = jnp.clip(0.2 + 0.8 * jax.random.uniform(arg_keys[13], (SEQS, SEQ, 2), jnp.float32) ** block_levels(arg_keys[13], (SEQS, SEQ, 2), ((0, 8), (1, 4)), -0.2, 0.2), 0.2, 1.0)
    return dict(x_in=x_in, z_gate=z_gate, b_proj=b_proj, c_proj=c_proj, decay_log=decay_log, skip_gain=skip_gain, residual=residual, ssd_gain=ssd_gain, moe_gain=moe_gain, w_gate=w_gate, w_up=w_up, w_down=w_down, routes=routes, route_weights=route_weights)


exact_mode = lax.Precision.HIGHEST

def group_carry(state, values, b_rows, running):
    remains = jnp.exp(running[-1][None, :] - running)
    fresh = jnp.einsum('jhp,jn->hpn', values * remains[:, :, None], b_rows, precision=exact_mode)
    return jnp.exp(running[-1])[:, None, None] * state + fresh

def group_step(state, inputs, skip_gain):
    values, b_rows, c_rows, log_rates = inputs
    length = values.shape[0]
    running = jnp.cumsum(log_rates, axis=0)
    across = running.T[:, :, None] - running.T[:, None, :]
    places = jnp.arange(length)
    causal = (places[:, None] >= places[None, :])[None]
    masked = jnp.where(causal, jnp.exp(jnp.where(causal, across, 0.0)), 0.0)
    scores = jnp.dot(c_rows, b_rows.T, precision=exact_mode)
    mixing = masked * scores[None]
    output = jnp.einsum('hij,jhp->ihp', mixing, values, precision=exact_mode)
    output = output + jnp.exp(running)[:, :, None] * jnp.einsum('in,hpn->ihp', c_rows, state, precision=exact_mode)
    output = output + skip_gain[None, :, None] * values
    return (group_carry(state, values, b_rows, running), output)

def sequence_scan(values, b_rows, c_rows, log_rates, skip_gain):
    length, heads, width = values.shape
    block = math.gcd(length, 256)
    count = length // block
    inputs = (values.reshape(count, block, heads, width), b_rows.reshape(count, block, -1), c_rows.reshape(count, block, -1), log_rates.reshape(count, block, heads))
    start = jnp.zeros((heads, width, b_rows.shape[1]), jnp.float32)
    _, outputs = lax.scan(lambda state, piece: group_step(state, piece, skip_gain), start, inputs)
    return outputs.reshape(length, heads * width)

def rms_scale(rows, gain):
    return gain * rows / jnp.sqrt(lax.optimization_barrier(jnp.mean(rows * rows, axis=-1, keepdims=True)) + 1e-05)

def expert_apply(rows, gate_mat, up_mat, down_mat):
    gate = jnp.dot(rows, gate_mat, preferred_element_type=jnp.float32)
    upper = jnp.dot(rows, up_mat, preferred_element_type=jnp.float32)
    hidden = (jax.nn.silu(gate) * upper).astype(jnp.bfloat16)
    return jnp.dot(hidden, down_mat, preferred_element_type=jnp.float32).astype(jnp.bfloat16)

def reference(x_in, z_gate, b_proj, c_proj, decay_log, skip_gain, residual, ssd_gain, moe_gain, w_gate, w_up, w_down, routes, route_weights):
    heads = skip_gain.shape[0]
    width = D // heads

    def one_sequence(item):
        return sequence_scan(item[0].reshape(SEQ, heads, width), item[1], item[2], item[3], skip_gain)
    mixed_ssd = lax.map(one_sequence, (x_in, b_proj, c_proj, decay_log))
    gated = mixed_ssd * jax.nn.silu(z_gate.astype(jnp.float32))
    hres = residual + rms_scale(gated, ssd_gain)
    normed = rms_scale(hres, moe_gain).astype(jnp.bfloat16)
    total = SEQS * SEQ
    flat_rows = normed.reshape(total, D)
    flat_routes = routes.reshape(total, 2)
    flat_weights = route_weights.reshape(total, 2)
    bound = min(total, total // L_DEV * CAP)

    def one_expert(index, accum):
        chosen = flat_routes == index
        member = jnp.any(chosen, axis=1)
        scale = lax.optimization_barrier(jnp.sum(jnp.where(chosen, flat_weights, 0.0), axis=1))
        picks = jnp.nonzero(member, size=bound, fill_value=0)[0]
        live = jnp.arange(bound) < jnp.sum(member.astype(jnp.int32))
        result = expert_apply(flat_rows[picks], w_gate[index], w_up[index], w_down[index]).astype(jnp.float32)
        result = result * jnp.where(live, scale[picks], 0.0)[:, None]
        return accum.at[picks].add(result)
    moe = lax.fori_loop(0, EXPERTS, one_expert, jnp.zeros((total, D), jnp.float32))
    return hres + moe.reshape(SEQS, SEQ, D)
```

```python
import jax
import jax.numpy as jnp
from jax import lax
from jax.sharding import Mesh
from jax.sharding import PartitionSpec as P

exact_mode = lax.Precision.HIGHEST

TM = ("zh", "zp")
EXPERT = ("col", "core")


def state_before(through, local_end):
    count = lax.axis_size(TM)

    def shifted(value, by):
        pairs = [(z, z + by) for z in range(count - by)]
        return lax.ppermute(value, TM, pairs)

    decay = shifted(through, 1)
    state = shifted(local_end.astype(jnp.bfloat16), 1).astype(jnp.float32)
    by = 1
    while by < count - 1:
        earlier = shifted(state.astype(jnp.bfloat16), by).astype(jnp.float32)
        state = decay[:, None, None] * earlier + state
        if 2 * by < count - 1:
            decay = decay * shifted(decay, by)
        by *= 2
    return state


def whole_expert(shard, exchange_axes):
    count = lax.axis_size(TM)
    place = lax.axis_index(TM)
    core = lax.axis_index("core")
    group = lax.axis_index("zh")
    rows, width = shard.shape
    half = rows // 2
    halves = shard.reshape(2, half, width)
    full = jnp.zeros((count, 2, half, width), shard.dtype)
    for turn in range(count):
        pairs = []
        for z in range(count):
            spot = (z + turn) % count
            for owned in range(2):
                pairs.append((z * 2 + owned, (owned + 2 * (spot // 2)) * 2 + spot % 2))
        wanted = lax.rem(place + turn, 2)
        piece = lax.dynamic_index_in_dim(halves, wanted, 0, keepdims=False)
        mine = lax.ppermute(piece, exchange_axes, pairs)
        other = lax.ppermute(mine, "core", [(0, 1), (1, 0)])
        origin = lax.rem(2 * group + core - turn + count, count)
        origin_other = lax.rem(2 * group + 1 - core - turn + count, count)
        full = lax.dynamic_update_slice(full, mine[None, None], (origin, core, 0, 0))
        full = lax.dynamic_update_slice(full, other[None, None], (origin_other, 1 - core, 0, 0))
    return full.reshape(count * rows, width)


def rms_scale(rows, gain):
    return gain * rows / jnp.sqrt(jnp.mean(rows * rows, axis=-1, keepdims=True) + 1e-05)


def per_device(
    x_in,
    z_gate,
    b_proj,
    c_proj,
    decay_log,
    skip_gain,
    residual,
    ssd_gain,
    moe_gain,
    w_gate,
    w_up,
    w_down,
    routes,
    route_weights,
):
    heads = skip_gain.shape[0]
    model_width = x_in.shape[2]
    width = model_width // heads
    length = x_in.shape[1]
    hidden_width = w_gate.shape[2]

    both = whole_expert(jnp.concatenate([w_gate[0], w_up[0]], axis=1), ("zh", "zp", "core"))
    down = whole_expert(w_down[0], ("zh", "zp", "core"))

    values = x_in[0].reshape(length, heads, width)
    b_rows = b_proj[0]
    c_rows = c_proj[0]
    running = jnp.cumsum(decay_log[0], axis=0)
    through = jnp.exp(running[-1])
    remains = jnp.exp(running[-1][None, :] - running)
    local_end = jnp.einsum(
        "jhp,jn->hpn", values * remains[:, :, None], b_rows, precision=exact_mode
    )
    incoming = state_before(through, local_end)

    across = running.T[:, :, None] - running.T[:, None, :]
    places = jnp.arange(length)
    causal = (places[:, None] >= places[None, :])[None]
    masked = jnp.where(causal, jnp.exp(jnp.where(causal, across, 0.0)), 0.0)
    scores = jnp.dot(c_rows, b_rows.T, precision=exact_mode)
    output = jnp.einsum("hij,jhp->ihp", masked * scores[None], values, precision=exact_mode)
    output = output + skip_gain[None, :, None] * values
    output = output + jnp.exp(running)[:, :, None] * jnp.einsum(
        "in,hpn->ihp", c_rows, incoming, precision=exact_mode
    )
    gated = output.reshape(length, model_width) * jax.nn.silu(z_gate[0].astype(jnp.float32))
    hres = residual[0] + rms_scale(gated, ssd_gain)
    normed = rms_scale(hres, moe_gain).astype(jnp.bfloat16)

    expert_count = lax.axis_size(EXPERT)
    capacity = max(2, 3 * length // expert_count)
    slot_rows = expert_count * capacity
    flat_routes = routes[0].reshape(-1)
    picked_one = (flat_routes[:, None] == jnp.arange(expert_count)[None, :]).astype(jnp.int32)
    earlier_hits = jnp.cumsum(picked_one, axis=0) - picked_one
    slot_index = jnp.sum(earlier_hits * picked_one, axis=1)
    block = (flat_routes % 2) * (expert_count // 2) + flat_routes // 2
    target = block * capacity + slot_index
    repeated = jnp.broadcast_to(normed[:, None, :], (length, 2, model_width)).reshape(
        2 * length, model_width
    )
    outgoing = jnp.zeros((slot_rows, model_width), jnp.bfloat16).at[target].set(repeated)
    received = lax.all_to_all(
        outgoing.reshape(expert_count, capacity, model_width),
        ("zp", "col"),
        split_axis=0,
        concat_axis=0,
        tiled=True,
    ).reshape(slot_rows, model_width)
    gate_up = jnp.dot(received, both, preferred_element_type=jnp.float32)
    hidden = (jax.nn.silu(gate_up[:, :hidden_width]) * gate_up[:, hidden_width:]).astype(
        jnp.bfloat16
    )
    produced = jnp.dot(hidden, down, preferred_element_type=jnp.float32).astype(jnp.bfloat16)
    back = lax.all_to_all(
        produced.reshape(expert_count, capacity, model_width),
        ("zp", "col"),
        split_axis=0,
        concat_axis=0,
        tiled=True,
    ).reshape(slot_rows, model_width)
    fetched = back[target].astype(jnp.float32).reshape(length, 2, model_width)
    weights_here = route_weights[0]
    moe = fetched[:, 0, :] * weights_here[:, 0:1] + fetched[:, 1, :] * weights_here[:, 1:2]
    return (hres + moe).reshape(1, length, model_width)


def solution(mesh):
    tm, expert = mesh.shape["tm"], mesh.shape["expert"]
    finer = Mesh(
        mesh.devices.reshape(tm // 2, 2, expert // 2, 2), ("zh", "zp", "col", "core")
    )
    split = P(EXPERT, TM, None)
    in_specs = tuple(P() if place in (5, 7, 8) else split for place in range(14))
    return jax.shard_map(
        per_device, mesh=finer, in_specs=in_specs, out_specs=split, check_vma=False
    )
```

```python
import jax
import jax.numpy as jnp
from jax import lax
from jax.sharding import Mesh
from jax.sharding import PartitionSpec as P

exact_mode = lax.Precision.HIGHEST

TM = ("zh", "zp")
EXPERT = ("col", "core")


def state_before(through, local_end):
    state = jnp.zeros_like(local_end)
    for place in range(lax.axis_size(TM) - 1):
        end = through[:, None, None] * state + local_end
        came = lax.ppermute(end.astype(jnp.bfloat16), TM, [(place, place + 1)])
        state = state + came.astype(jnp.float32)
    return state


def sent_rows(shard, after):
    count = lax.axis_size(TM)
    place = lax.axis_index(TM)
    half = shard.shape[0] // 2
    arrived = []
    for turn in range(count):
        pairs = []
        for z in range(count):
            spot = (z + turn) % count
            for owned in range(2):
                pairs.append((z * 2 + owned, (owned + 2 * (spot // 2)) * 2 + spot % 2))
        wanted = lax.rem(place + turn, 2)
        piece = lax.dynamic_slice(shard, (wanted * half, 0), (half, shard.shape[1]))
        if after is not None:
            piece, _ = lax.optimization_barrier((piece, after[turn]))
        arrived.append(lax.ppermute(piece, ("zh", "zp", "core"), pairs))
    return arrived


def joined_rows(arrived):
    count = lax.axis_size(TM)
    core = lax.axis_index("core")
    group = lax.axis_index("zh")
    half, width = arrived[0].shape
    full = jnp.zeros((count, 2, half, width), arrived[0].dtype)
    for turn in range(count):
        other = lax.ppermute(arrived[turn], "core", [(0, 1), (1, 0)])
        for piece, side in ((arrived[turn], core), (other, 1 - core)):
            origin = lax.rem(2 * group + side - turn + count, count)
            full = lax.dynamic_update_slice(full, piece[None, None], (origin, side, 0, 0))
    return full.reshape(count * 2 * half, width)


def rms_scale(rows, gain):
    return gain * rows / jnp.sqrt(jnp.mean(rows * rows, axis=-1, keepdims=True) + 1e-05)


def per_device(
    x_in,
    z_gate,
    b_proj,
    c_proj,
    decay_log,
    skip_gain,
    residual,
    ssd_gain,
    moe_gain,
    w_gate,
    w_up,
    w_down,
    routes,
    route_weights,
):
    heads = skip_gain.shape[0]
    model_width = x_in.shape[2]
    width = model_width // heads
    length = x_in.shape[1]
    hidden_width = w_gate.shape[2]

    wide_pieces = sent_rows(jnp.concatenate([w_gate[0], w_up[0]], axis=1), None)
    down_pieces = sent_rows(w_down[0], wide_pieces)
    both = joined_rows(wide_pieces)
    down = joined_rows(down_pieces)

    values = x_in[0].reshape(length, heads, width)
    b_rows = b_proj[0]
    c_rows = c_proj[0]
    running = jnp.cumsum(decay_log[0], axis=0)
    through = jnp.exp(running[-1])
    remains = jnp.exp(running[-1][None, :] - running)
    local_end = jnp.einsum(
        "jhp,jn->hpn", values * remains[:, :, None], b_rows, precision=exact_mode
    )
    incoming = state_before(through, local_end)

    across = running.T[:, :, None] - running.T[:, None, :]
    places = jnp.arange(length)
    causal = (places[:, None] >= places[None, :])[None]
    masked = jnp.where(causal, jnp.exp(jnp.where(causal, across, 0.0)), 0.0)
    scores = jnp.dot(c_rows, b_rows.T, precision=exact_mode)
    output = jnp.einsum("hij,jhp->ihp", masked * scores[None], values, precision=exact_mode)
    output = output + skip_gain[None, :, None] * values
    output = output + jnp.exp(running)[:, :, None] * jnp.einsum(
        "in,hpn->ihp", c_rows, incoming, precision=exact_mode
    )
    gated = output.reshape(length, model_width) * jax.nn.silu(z_gate[0].astype(jnp.float32))
    hres = residual[0] + rms_scale(gated, ssd_gain)
    normed = rms_scale(hres, moe_gain).astype(jnp.bfloat16)

    expert_count = lax.axis_size(EXPERT)
    capacity = max(2, 3 * length // expert_count)
    slot_rows = expert_count * capacity
    flat_routes = routes[0].reshape(-1)
    picked_one = (flat_routes[:, None] == jnp.arange(expert_count)[None, :]).astype(jnp.int32)
    earlier_hits = jnp.cumsum(picked_one, axis=0) - picked_one
    slot_index = jnp.sum(earlier_hits * picked_one, axis=1)
    block = (flat_routes % 2) * (expert_count // 2) + flat_routes // 2
    target = block * capacity + slot_index
    repeated = jnp.broadcast_to(normed[:, None, :], (length, 2, model_width)).reshape(
        2 * length, model_width
    )
    outgoing = jnp.zeros((slot_rows, model_width), jnp.bfloat16).at[target].set(repeated)
    received = lax.all_to_all(
        outgoing.reshape(expert_count, capacity, model_width),
        ("zp", "col"),
        split_axis=0,
        concat_axis=0,
        tiled=True,
    ).reshape(slot_rows, model_width)
    gate_up = jnp.dot(received, both, preferred_element_type=jnp.float32)
    hidden = (jax.nn.silu(gate_up[:, :hidden_width]) * gate_up[:, hidden_width:]).astype(
        jnp.bfloat16
    )
    produced = jnp.dot(hidden, down, preferred_element_type=jnp.float32).astype(jnp.bfloat16)
    back = lax.all_to_all(
        produced.reshape(expert_count, capacity, model_width),
        ("zp", "col"),
        split_axis=0,
        concat_axis=0,
        tiled=True,
    ).reshape(slot_rows, model_width)
    fetched = back[target].astype(jnp.float32).reshape(length, 2, model_width)
    weights_here = route_weights[0]
    moe = fetched[:, 0, :] * weights_here[:, 0:1] + fetched[:, 1, :] * weights_here[:, 1:2]
    return (hres + moe).reshape(1, length, model_width)


def solution(mesh):
    tm, expert = mesh.shape["tm"], mesh.shape["expert"]
    finer = Mesh(
        mesh.devices.reshape(tm // 2, 2, expert // 2, 2), ("zh", "zp", "col", "core")
    )
    split = P(EXPERT, TM, None)
    in_specs = tuple(P() if place in (5, 7, 8) else split for place in range(14))
    return jax.shard_map(
        per_device, mesh=finer, in_specs=in_specs, out_specs=split, check_vma=False
    )
```
